32 devices in a mesh: segment: 2 (over core), dp: 8 (over z, y), tensor: 2 (over x).
Axes of the slice: x: 2, y: 2, z: 4, core: 2. Of those that a mesh axis runs over, the one named last changes fastest.
Arguments:
- tokens: bfloat16 [256, 5120], P('dp'), may hold values from -12 to 12
- cotangent: bfloat16 [256, 5120], P('dp'), may hold values from -6 to 6
- gains: float32 [2, 5120], P('segment'), may hold values from 0.1 to 1.9
- w_gate: bfloat16 [2, 5120, 27648], P('segment', 'dp', 'tensor'), may hold values from -0.078125 to 0.078125
- w_up: bfloat16 [2, 5120, 27648], P('segment', 'dp', 'tensor'), may hold values from -0.078125 to 0.078125
- w_down: bfloat16 [2, 5120, 27648], P('segment', 'dp', 'tensor'), may hold values from -0.0390625 to 0.0390625
Outputs:
- acts: bfloat16 [2, 256, 5120], P('segment', 'dp')
- grads: bfloat16 [2, 256, 5120], P('segment', 'dp')
The draws below stay inside these ranges and needn't reach their ends.
All inputs are finite; a program needn't handle non-finite values.
Results may differ from the reference program's by a relative error of at most 0.04.
Values may be sent and summed in bfloat16 or wider, within the bound.
No kernel may reach another device: no remote copies, remote signals or barrier semaphores. Data moves between devices by JAX's collectives and lax.ppermute only.
A program may use at most 128 MiB of HBM per device.

```python
import math
import jax
import jax.numpy as jnp
from jax import lax

D = 5120
FF = 27648
TOKENS = 256
N_DP = 8


def draw_tokens(key, part):
    noise_key, row_key = jax.random.split(key, 2)
    row_scale = jnp.exp(jax.random.uniform(row_key, (TOKENS, 1), jnp.float32, math.log(0.3), math.log(3.0)))
    noise_values = jnp.clip(jax.random.normal(noise_key, (TOKENS, D), jnp.float32), -4.0, 4.0)
    return (noise_values * row_scale).astype(jnp.bfloat16)


def level_of(stream_key, dims, cuts, least, top_value):
    def one(dim, shards_of):
        draws = jax.random.uniform(jax.random.fold_in(jax.random.fold_in(stream_key, 6), dim), (shards_of,), jnp.float32, least / len(cuts), top_value / len(cuts))
        return jnp.repeat(jnp.exp(draws), dims[dim] // shards_of).reshape((-1,) + (1,) * (len(dims) - dim - 1))

    gain = one(*cuts[0])
    for cut in cuts[1:]:
        gain = gain * one(*cut)
    return gain


def scatter_about(stream_key, shape, scale, most, pieces=(), held_as=jnp.bfloat16):
    values = scale * jax.random.normal(stream_key, shape, jnp.float32)
    if pieces:
        values = values * level_of(stream_key, shape, pieces, -0.22, 0.18)
    return jnp.clip(values, -most, most).astype(held_as)


def setup_inputs(seed: int = 0) -> dict:
    seeds = jax.random.split(jax.random.key(seed), 7)
    tokens = draw_tokens(jax.random.fold_in(seeds[6], 71), 0)
    cotangent = scatter_about(seeds[1], (TOKENS, D), 1.0, 6.0, ((0, 8),))
    gains = jnp.clip(1.0 + 0.18 * jax.random.normal(seeds[2], (2, D), jnp.float32), 0.1, 1.9)
    w_gate = scatter_about(seeds[3], (2, D, FF), D ** -0.5, 0.078125, ((0, 2), (1, 8), (2, 2)))
    w_up = scatter_about(seeds[4], (2, D, FF), D ** -0.5, 0.078125, ((0, 2), (1, 8), (2, 2)))
    w_down = scatter_about(seeds[5], (2, D, FF), FF ** -0.5, 0.0390625, ((0, 2), (1, 8), (2, 2)))
    return dict(tokens=tokens, cotangent=cotangent, gains=gains, w_gate=w_gate, w_up=w_up, w_down=w_down)


EPSILON = 1e-06

def normalize(values):
    wide = values.astype(jnp.float32)
    inverse = lax.rsqrt(lax.optimization_barrier(jnp.mean(wide * wide, axis=1, keepdims=True)) + EPSILON)
    return (wide, wide * inverse, inverse)

def contract_last(left, right):
    return lax.dot_general(left, right, (((1,), (1,)), ((), ())), preferred_element_type=jnp.float32)

def blocked_product(left, right):
    width = left.shape[1] // N_DP
    total = jnp.zeros((left.shape[0], right.shape[1]), jnp.float32)
    for block in range(N_DP):
        piece = jnp.dot(left[:, block * width:(block + 1) * width], right[block * width:(block + 1) * width, :], preferred_element_type=jnp.float32)
        rounded = lax.optimization_barrier(piece.astype(jnp.bfloat16))
        total = total + rounded.astype(jnp.float32)
    return total

def sublayer_forward(values, gain_row, gate_weight, up_weight, down_weight):
    wide, unit, inverse = normalize(values)
    normed = (unit * gain_row[None, :]).astype(jnp.bfloat16)
    gate_pre = blocked_product(normed, gate_weight)
    up_pre = blocked_product(normed, up_weight)
    hidden = (jax.nn.silu(gate_pre) * up_pre).astype(jnp.bfloat16)
    branch_out = contract_last(hidden, down_weight)
    return ((wide + branch_out).astype(jnp.bfloat16), gate_pre.astype(jnp.bfloat16), up_pre.astype(jnp.bfloat16))

def sublayer_backward(values, gain_row, gate_weight, up_weight, down_weight, stash_gate, stash_up, incoming):
    wide, unit, inverse = normalize(values)
    d_hidden = blocked_product(incoming, down_weight)
    gate_pre = stash_gate.astype(jnp.float32)
    up_pre = stash_up.astype(jnp.float32)
    sigmoid_gate = jax.nn.sigmoid(gate_pre)
    d_gate = (d_hidden * up_pre * sigmoid_gate * (1.0 + gate_pre * (1.0 - sigmoid_gate))).astype(jnp.bfloat16)
    d_up = (d_hidden * gate_pre * sigmoid_gate).astype(jnp.bfloat16)
    d_normed = contract_last(d_gate, gate_weight) + contract_last(d_up, up_weight)
    weighted = d_normed * gain_row[None, :]
    projection = lax.optimization_barrier(jnp.mean(weighted * unit, axis=1, keepdims=True))
    return (incoming.astype(jnp.float32) + inverse * (weighted - unit * projection)).astype(jnp.bfloat16)

def reference(tokens, cotangent, gains, w_gate, w_up, w_down):
    early_out, early_gate, early_up = sublayer_forward(tokens, gains[0], w_gate[0], w_up[0], w_down[0])
    late_out, late_gate, late_up = sublayer_forward(early_out, gains[1], w_gate[1], w_up[1], w_down[1])
    d_early = sublayer_backward(early_out, gains[1], w_gate[1], w_up[1], w_down[1], late_gate, late_up, cotangent)
    d_tokens = sublayer_backward(tokens, gains[0], w_gate[0], w_up[0], w_down[0], early_gate, early_up, d_early)
    return (jnp.stack([early_out, late_out]), jnp.stack([d_tokens, d_early]))
```

```python
import jax
import jax.numpy as jnp
from jax import lax
from jax.sharding import PartitionSpec as P

EPSILON = 1e-06
BF16 = jnp.bfloat16
F32 = jnp.float32

GATHER_SHARE = 0.5
SCATTER_SHARE = 0.5
PAIR_FIRST = 2 / 3


def cut(width, share):
    lanes = 128
    whole = width // lanes
    return min(max(int(whole * share + 0.5), 1), whole - 1) * lanes


def contract_last(left, right):
    return lax.dot_general(left, right, (((1,), (1,)), ((), ())), preferred_element_type=F32)


def dot(left, right):
    return jnp.dot(left, right, preferred_element_type=F32)


def swap(value, axis, step=1):
    count = lax.axis_size(axis)
    return lax.ppermute(value, axis, [(i, i ^ step) for i in range(count)])


def line_groups():
    count = lax.axis_size("dp")
    return [list(range(start, count, 2)) for start in range(2)]


def line_exchange(value, axis):
    return lax.all_to_all(
        value, "dp", split_axis=axis, concat_axis=axis, tiled=True, axis_index_groups=line_groups()
    )


def pair_relative(value):
    count = lax.axis_size("dp")
    split = value.reshape((count // 2, 2, value.shape[0] // count) + value.shape[1:])
    own_first = jnp.where(lax.axis_index("dp") % 2 == 0, split, split[:, ::-1])
    return own_first.reshape(value.shape)


def scatter_call(value):
    return lax.psum_scatter(value, "dp", scatter_dimension=0, tiled=True).astype(F32)


def scatter_hops(value):
    count = lax.axis_size("dp")
    rows = value.shape[0] // count
    width = value.shape[1]
    split = value.reshape(count // 2, 2, rows, width)
    edge = cut(width, PAIR_FIRST)
    first, second = split[..., :edge], split[..., edge:]
    first_in = swap(first[:, 1], "dp")
    second_sum = jnp.sum(line_exchange(second, 0).astype(F32), axis=0).astype(BF16)
    first_sum = (first[:, 0].astype(F32) + first_in.astype(F32)).astype(BF16)
    second_in = swap(second_sum[1], "dp")
    first_out = jnp.sum(line_exchange(first_sum, 0).astype(F32), axis=0)
    second_out = second_sum[0].astype(F32) + second_in.astype(F32)
    return jnp.concatenate([first_out, second_out], axis=1)


def gather_call(value):
    return lax.all_gather(value, "dp", axis=0, tiled=True)


def gather_hops(value):
    count = lax.axis_size("dp")
    rows, width = value.shape
    edge = cut(width, PAIR_FIRST)

    def spread(part):
        return line_exchange(jnp.broadcast_to(part[None], (count // 2,) + part.shape), 0)

    first, second = value[:, :edge], value[:, edge:]
    second_pair = jnp.stack([second, swap(second, "dp")])
    first_line = spread(first)
    second_all = spread(second_pair)
    first_all = jnp.stack([first_line, swap(first_line, "dp")], axis=1)
    return (
        first_all.reshape(count * rows, edge),
        second_all.reshape(count * rows, width - edge),
    )


def sum_shares(partial_value):
    total = partial_value.astype(BF16)
    total = (total.astype(F32) + swap(total, "segment").astype(F32)).astype(BF16)
    step = 1
    while step < lax.axis_size("tensor"):
        wide = total.astype(F32) + swap(total, "tensor", step).astype(F32)
        step *= 2
        total = wide.astype(BF16) if step < lax.axis_size("tensor") else wide
    return total.astype(F32)


def input_grads(d_hidden, stash_gate, stash_up):
    gate_pre = stash_gate.astype(F32)
    up_pre = stash_up.astype(F32)
    sigmoid_gate = jax.nn.sigmoid(gate_pre)
    d_gate = (d_hidden * up_pre * sigmoid_gate * (1.0 + gate_pre * (1.0 - sigmoid_gate))).astype(BF16)
    d_up = (d_hidden * gate_pre * sigmoid_gate).astype(BF16)
    return (d_gate, d_up)


def body(tokens, cotangent, gains, w_gate, w_up, w_down):
    gate_weight, up_weight, down_weight = w_gate[0], w_up[0], w_down[0]
    column_block, held = gate_weight.shape
    half = held // 2
    rows, features = tokens.shape
    segment = lax.axis_index("segment")
    block = lax.axis_index("dp")
    leading = segment == 0

    def other_half(weight):
        given = lax.dynamic_slice_in_dim(weight, (1 - segment) * half, half, 1)
        return swap(given, "segment")

    gate_other, up_other, down_other = (
        other_half(gate_weight),
        other_half(up_weight),
        other_half(down_weight),
    )

    def early(function, own, other, value):
        return lax.cond(
            leading,
            lambda v, mine, theirs: function(v, mine[:, :half]),
            lambda v, mine, theirs: function(v, theirs),
            value,
            own,
            other,
        )

    def late(function, own, other, value):
        return lax.cond(
            leading,
            lambda v, mine, theirs: function(v, theirs),
            lambda v, mine, theirs: function(v, mine[:, half:]),
            value,
            own,
            other,
        )

    def product(value, weight):
        return dot(value, weight).astype(BF16)

    def own_rows(value):
        return lax.dynamic_slice_in_dim(value, block * rows, rows, 0)

    def to_rows(value):
        return lax.all_to_all(value, "dp", split_axis=0, concat_axis=1, tiled=True)

    mixed = lax.all_to_all(
        jnp.where(leading, tokens, cotangent), "dp", split_axis=1, concat_axis=0, tiled=True
    )
    mixed_other = swap(mixed, "segment")
    token_cols = jnp.where(leading, mixed, mixed_other)
    cotangent_cols = jnp.where(leading, mixed_other, mixed)
    gain_own = lax.dynamic_slice_in_dim(gains, block * column_block, column_block, 1)
    gain_other = swap(gain_own, "segment")
    early_gain = jnp.where(leading, gain_own, gain_other)
    late_gain = jnp.where(leading, gain_other, gain_own)

    wide_tokens = tokens.astype(F32)
    inverse_in = lax.rsqrt(jnp.mean(wide_tokens * wide_tokens, axis=1, keepdims=True) + EPSILON)

    def hidden_inputs(apply, cols, gain_row, inverse):
        scaled = (cols.astype(F32) * gain_row).astype(BF16)
        gate_part = apply(product, gate_weight, gate_other, scaled)
        up_part = apply(product, up_weight, up_other, pair_relative(scaled))
        return scatter_call(gate_part), scatter_hops(up_part)

    def down_product(apply, hidden):
        edge = cut(half, GATHER_SHARE)
        called = gather_call(hidden[:, :edge])
        hop_a, hop_b = gather_hops(hidden[:, edge:])
        mid = edge + hop_a.shape[1]

        def natural(v, w):
            return contract_last(v, w[:, :edge])

        def relative(v, w):
            return contract_last(v[0], w[:, edge:mid]) + contract_last(v[1], w[:, mid:])

        return apply(natural, down_weight, down_other, called) + pair_relative(
            apply(relative, down_weight, down_other, (hop_a, hop_b))
        )

    def normed_grads(apply, d_gate, d_up):
        called = gather_call(d_gate)
        hop_a, hop_b = gather_hops(d_up)
        edge = hop_a.shape[1]

        def relative(v, w):
            return contract_last(v[0], w[:, :edge]) + contract_last(v[1], w[:, edge:])

        return apply(contract_last, gate_weight, gate_other, called) + pair_relative(
            apply(relative, up_weight, up_other, (hop_a, hop_b))
        )

    def projection(d_gate, d_up, gate, up):
        mine = jnp.sum(d_gate.astype(F32) * gate + d_up.astype(F32) * up, axis=1)
        everyone = lax.all_gather(mine, ("segment", "dp", "tensor"))
        shape = (lax.axis_size("segment"), lax.axis_size("dp"), lax.axis_size("tensor"), rows)
        return jnp.sum(everyone.reshape(shape), axis=(0, 2)).reshape(-1, 1) / features

    def norm_back(cols, inverse, gain_row, d_normed, mean_value, incoming):
        unit = cols.astype(F32) * inverse
        weighted = d_normed * gain_row
        return (incoming.astype(F32) + inverse * (weighted - unit * mean_value)).astype(BF16)

    gate_sum, up_sum = hidden_inputs(early, token_cols, early_gain, inverse_in)
    early_gate, early_up = gate_sum * inverse_in, up_sum * inverse_in
    stash_gate, stash_up = early_gate.astype(BF16), early_up.astype(BF16)
    early_hidden = (jax.nn.silu(early_gate) * early_up).astype(BF16)
    late_d_hidden = scatter_call(late(product, down_weight, down_other, cotangent_cols))
    inverse_all = lax.all_gather(inverse_in, "dp", axis=0, tiled=True)
    early_out = (
        token_cols.astype(F32) + sum_shares(down_product(early, early_hidden))
    ).astype(BF16)

    wide_mid = early_out.astype(F32)
    squares = lax.all_gather(jnp.sum(wide_mid * wide_mid, axis=1), "dp")
    inverse_mid = lax.rsqrt(jnp.sum(squares, axis=0)[:, None] / features + EPSILON)
    gate_sum, up_sum = hidden_inputs(late, early_out, late_gain, inverse_mid)
    inverse_own = own_rows(inverse_mid)
    late_gate, late_up = gate_sum * inverse_own, up_sum * inverse_own
    late_hidden = (jax.nn.silu(late_gate) * late_up).astype(BF16)
    d_gate, d_up = input_grads(late_d_hidden, late_gate.astype(BF16), late_up.astype(BF16))
    mean_value = projection(d_gate, d_up, late_gate, late_up)
    d_normed = sum_shares(normed_grads(late, d_gate, d_up))
    d_early = norm_back(early_out, inverse_mid, late_gain, d_normed, mean_value, cotangent_cols)
    late_out = (wide_mid + sum_shares(down_product(late, late_hidden))).astype(BF16)
    acts = to_rows(jnp.where(leading, early_out, late_out))[None]

    edge = cut(half, SCATTER_SHARE)
    d_hidden = jnp.concatenate(
        [
            scatter_call(early(lambda v, w: product(v, w[:, :edge]), down_weight, down_other, d_early)),
            scatter_hops(
                early(
                    lambda v, w: product(v, w[:, edge:]),
                    down_weight,
                    down_other,
                    pair_relative(d_early),
                )
            ),
        ],
        axis=1,
    )
    d_gate, d_up = input_grads(d_hidden, stash_gate, stash_up)
    mean_value = projection(d_gate, d_up, early_gate, early_up)
    d_normed = sum_shares(normed_grads(early, d_gate, d_up))
    d_tokens = norm_back(token_cols, inverse_all, early_gain, d_normed, mean_value, d_early)
    grads = to_rows(jnp.where(leading, d_tokens, d_early))[None]
    return (acts, grads)


def solution(mesh):
    in_specs = (
        P("dp", None),
        P("dp", None),
        P("segment", None),
        P("segment", "dp", "tensor"),
        P("segment", "dp", "tensor"),
        P("segment", "dp", "tensor"),
    )
    out_specs = (P("segment", "dp", None), P("segment", "dp", None))
    return jax.shard_map(body, mesh=mesh, in_specs=in_specs, out_specs=out_specs, check_vma=False)
```

```python
import jax
import jax.numpy as jnp
from jax import lax
from jax.sharding import PartitionSpec as P

EPSILON = 1e-06
BF16 = jnp.bfloat16
F32 = jnp.float32
LANES = 128

GATE_SHARE = 1.0
UP_SHARE = 0.0
EARLY_HIDDEN_SHARE = 1.0
LATE_HIDDEN_SHARE = 1.0
EARLY_BACK_SHARE = 0.0
LATE_BACK_SHARE = 0.0
HOP_PIECES = 2


def cut(width, share):
    if share <= 0.0:
        return 0
    if share >= 1.0:
        return width
    whole = width // LANES
    return min(max(int(whole * share + 0.5), 1), whole - 1) * LANES


def pieces_of(low, high, count):
    units = (high - low) // LANES
    count = max(1, min(count, units))
    edges = [low + LANES * (units * i // count) for i in range(count)] + [high]
    return list(zip(edges[:-1], edges[1:]))


def contract_last(left, right):
    return lax.dot_general(left, right, (((1,), (1,)), ((), ())), preferred_element_type=F32)


def product(left, right):
    return jnp.dot(left, right, preferred_element_type=F32).astype(BF16)


def swap(value, axis, step=1):
    count = lax.axis_size(axis)
    return lax.ppermute(value, axis, [(i, i ^ step) for i in range(count)])


def line_exchange(value):
    count = lax.axis_size("dp")
    groups = [list(range(start, count, 2)) for start in range(2)]
    return lax.all_to_all(
        value, "dp", split_axis=0, concat_axis=0, tiled=True, axis_index_groups=groups
    )


def is_first_of_pair():
    return lax.axis_index("dp") % 2 == 0


def to_relative(value):
    count = lax.axis_size("dp")
    split = value.reshape((count // 2, 2, value.shape[0] // count) + value.shape[1:])
    flat = (value.shape[0] // 2,) + value.shape[1:]
    first, second = split[:, 0].reshape(flat), split[:, 1].reshape(flat)
    here = is_first_of_pair()
    return jnp.where(here, first, second), jnp.where(here, second, first)


def from_relative(own, other):
    count = lax.axis_size("dp")
    here = is_first_of_pair()
    shape = (count // 2, own.shape[0] // (count // 2)) + own.shape[1:]
    first = jnp.where(here, own, other).reshape(shape)
    second = jnp.where(here, other, own).reshape(shape)
    return jnp.stack([first, second], axis=1).reshape((2 * own.shape[0],) + own.shape[1:])


def scatter_product(multiply, values, width, share, marks=None, before=None):
    half_count = lax.axis_size("dp") // 2
    edge = cut(width, share)
    outs = []
    if edge > 0:
        part = multiply(values, 0, edge)
        if marks is not None:
            marks.append(part)
        if before is not None:
            part, before = lax.optimization_barrier((part, before))
        outs.append(lax.psum_scatter(part, "dp", scatter_dimension=0, tiled=True).astype(F32))
    if edge < width:
        own, other = to_relative(values)
        for low, high in pieces_of(edge, width, HOP_PIECES):
            given = multiply(other, low, high)
            kept = lax.optimization_barrier(multiply(own, low, high))
            if marks is not None:
                marks.append(kept)
            paired = (kept.astype(F32) + swap(given, "dp").astype(F32)).astype(BF16)
            lined = line_exchange(paired.reshape(half_count, -1, high - low))
            outs.append(jnp.sum(lined.astype(F32), axis=0))
    return jnp.concatenate(outs, axis=1) if len(outs) > 1 else outs[0]


def gather_contract(multiply, value, share, extra=None, first=None, marks=None):
    half_count = lax.axis_size("dp") // 2
    width = value.shape[1]
    edge = cut(width, share)
    total = None
    everyone = None
    if edge < width:
        own_total, other_total = None, None
        for low, high in pieces_of(edge, width, HOP_PIECES):
            part = value[:, low:high]
            if extra is not None and low == edge:
                part = jnp.concatenate([part, extra], axis=1)
            lined = line_exchange(jnp.broadcast_to(part[None], (half_count,) + part.shape))
            lined = lined.reshape(-1, part.shape[1])
            arrived = swap(lined, "dp")
            if extra is not None and low == edge:
                everyone = from_relative(lined[:, high - low :], arrived[:, high - low :])
                lined, arrived = lined[:, : high - low], arrived[:, : high - low]
            own_part = multiply(lined, low, high)
            if first is not None and high == width:
                arrived, first = lax.optimization_barrier((arrived, first))
            other_part = multiply(arrived, low, high)
            own_total = own_part if own_total is None else own_total + own_part
            other_total = other_part if other_total is None else other_total + other_part
        total = from_relative(own_total, other_total)
    if edge > 0:
        part = value[:, :edge]
        if extra is not None and edge == width:
            part = jnp.concatenate([part, extra], axis=1)
        called = lax.all_gather(part, "dp", axis=0, tiled=True)
        if marks is not None:
            marks.append(called)
        if extra is not None and edge == width:
            everyone = called[:, edge:]
        called = multiply(called[:, :edge], 0, edge)
        total = called if total is None else total + called
    if first is not None:
        total = total + first
    return total, everyone


def halving_sum(value, axis):
    step = 1
    while step < lax.axis_size(axis):
        value = value + swap(value, axis, step)
        step *= 2
    return value


def sum_shares(partial_value):
    total = partial_value.astype(BF16)
    total = (total.astype(F32) + swap(total, "segment").astype(F32)).astype(BF16)
    step = 1
    while step < lax.axis_size("tensor"):
        total = (total.astype(F32) + swap(total, "tensor", step).astype(F32)).astype(BF16)
        step *= 2
    return total.astype(F32)


def input_grads(d_hidden, stash_gate, stash_up):
    gate_pre = stash_gate.astype(F32)
    up_pre = stash_up.astype(F32)
    sigmoid_gate = jax.nn.sigmoid(gate_pre)
    d_gate = (d_hidden * up_pre * sigmoid_gate * (1.0 + gate_pre * (1.0 - sigmoid_gate))).astype(BF16)
    d_up = (d_hidden * gate_pre * sigmoid_gate).astype(BF16)
    return (d_gate, d_up)


def body(tokens, cotangent, gains, w_gate, w_up, w_down):
    gate_weight, up_weight, down_weight = w_gate[0], w_up[0], w_down[0]
    column_block, held = gate_weight.shape
    half = held // 2
    rows, features = tokens.shape
    segment = lax.axis_index("segment")
    block = lax.axis_index("dp")
    leading = segment == 0

    def other_half(weight, position):
        given = lax.dynamic_slice_in_dim(weight, (1 - position) * half, half, 1)
        return swap(given, "segment")

    def half_pick(own, other, early, function):
        def apply(value, low, high):
            first = lambda v, mine, theirs: function(v, mine, low, high)
            if early:
                return lax.cond(
                    leading, first, lambda v, m, t: function(v, t, low, high), value, own, other
                )
            return lax.cond(
                leading,
                lambda v, m, t: function(v, t, low, high),
                lambda v, m, t: function(v, m, half + low, half + high),
                value,
                own,
                other,
            )

        return apply

    def columns_product(value, weight, low, high):
        return product(value, weight[:, low:high])

    def columns_contract(value, weight, low, high):
        return contract_last(value, weight[:, low:high])

    def own_rows(value):
        return lax.dynamic_slice_in_dim(value, block * rows, rows, 0)

    def to_rows(value):
        return lax.all_to_all(value, "dp", split_axis=0, concat_axis=1, tiled=True)

    def row_inverse(cols):
        wide = cols.astype(F32)
        total = halving_sum(jnp.sum(wide * wide, axis=1), "dp")
        return lax.rsqrt(total[:, None] / features + EPSILON)

    gate_other = other_half(gate_weight, segment)
    up_other = other_half(up_weight, segment)
    mixed = lax.all_to_all(
        jnp.where(leading, tokens, cotangent), "dp", split_axis=1, concat_axis=0, tiled=True
    )
    mixed_other = swap(mixed, "segment")
    token_cols = jnp.where(leading, mixed, mixed_other)
    cotangent_cols = jnp.where(leading, mixed_other, mixed)
    gain_own = lax.dynamic_slice_in_dim(gains, block * column_block, column_block, 1)
    gain_other = swap(gain_own, "segment")
    early_gain = jnp.where(leading, gain_own, gain_other)
    late_gain = jnp.where(leading, gain_other, gain_own)

    def gate_and_up(early, cols, gain_row, marks=None):
        scaled = (cols.astype(F32) * gain_row).astype(BF16)
        gate = scatter_product(
            half_pick(gate_weight, gate_other, early, columns_product), scaled, half, GATE_SHARE, marks
        )
        up = scatter_product(
            half_pick(up_weight, up_other, early, columns_product), scaled, half, UP_SHARE, marks
        )
        return gate, up

    def hidden_of(gate, up):
        return (jax.nn.silu(gate) * up).astype(BF16)

    def back(early, d_hidden, gate, up):
        d_gate, d_up = input_grads(d_hidden, gate.astype(BF16), up.astype(BF16))
        share = jnp.sum(d_gate.astype(F32) * gate + d_up.astype(F32) * up, axis=1, keepdims=True)
        high = share.astype(BF16)
        low = (share - high.astype(F32)).astype(BF16)
        extra = jnp.pad(jnp.concatenate([high, low], axis=1), ((0, 0), (0, LANES - 2)))
        by_gate, _ = gather_contract(
            half_pick(gate_weight, gate_other, early, columns_contract), d_gate, GATE_SHARE
        )
        d_normed, everyone = gather_contract(
            half_pick(up_weight, up_other, early, columns_contract), d_up, UP_SHARE, extra, by_gate
        )
        shares = jnp.sum(everyone[:, :2].astype(F32), axis=1)
        mean_value = halving_sum(halving_sum(shares, "segment"), "tensor")[:, None] / features
        return d_normed, mean_value

    def norm_back(cols, inverse, gain_row, d_normed, mean_value, incoming):
        unit = cols.astype(F32) * inverse
        weighted = d_normed * gain_row
        return (incoming.astype(F32) + inverse * (weighted - unit * mean_value)).astype(BF16)

    inverse_in = row_inverse(token_cols)
    marks = []
    early_gate, early_up = gate_and_up(True, token_cols, early_gain, marks)
    after, _ = lax.optimization_barrier((segment, tuple(marks)))
    down_other = other_half(down_weight, after)
    late_d_hidden = scatter_product(
        half_pick(down_weight, down_other, False, columns_product),
        cotangent_cols,
        half,
        LATE_BACK_SHARE,
    )
    early_gate, early_up = early_gate * own_rows(inverse_in), early_up * own_rows(inverse_in)
    down_out, _ = gather_contract(
        half_pick(down_weight, down_other, True, columns_contract),
        hidden_of(early_gate, early_up),
        EARLY_HIDDEN_SHARE,
    )
    early_out = (token_cols.astype(F32) + sum_shares(down_out)).astype(BF16)
    early_out, late_d_hidden = lax.optimization_barrier((early_out, late_d_hidden))

    inverse_mid = row_inverse(early_out)
    late_gate, late_up = gate_and_up(False, early_out, late_gain)
    late_gate, late_up = late_gate * own_rows(inverse_mid), late_up * own_rows(inverse_mid)
    d_normed, mean_value = back(False, late_d_hidden, late_gate, late_up)
    down_out, _ = gather_contract(
        half_pick(down_weight, down_other, False, columns_contract),
        hidden_of(late_gate, late_up),
        LATE_HIDDEN_SHARE,
        marks=marks,
    )
    d_early = norm_back(
        early_out, inverse_mid, late_gain, sum_shares(d_normed), mean_value, cotangent_cols
    )
    late_out = (early_out.astype(F32) + sum_shares(down_out)).astype(BF16)
    acts = to_rows(jnp.where(leading, early_out, late_out))[None]

    d_hidden = scatter_product(
        half_pick(down_weight, down_other, True, columns_product),
        d_early,
        half,
        EARLY_BACK_SHARE,
        before=marks[-1],
    )
    d_normed, mean_value = back(True, d_hidden, early_gate, early_up)
    d_tokens = norm_back(
        token_cols, inverse_in, early_gain, sum_shares(d_normed), mean_value, d_early
    )
    grads = to_rows(jnp.where(leading, d_tokens, d_early))[None]
    return (acts, grads)


def solution(mesh):
    in_specs = (
        P("dp", None),
        P("dp", None),
        P("segment", None),
        P("segment", "dp", "tensor"),
        P("segment", "dp", "tensor"),
        P("segment", "dp", "tensor"),
    )
    out_specs = (P("segment", "dp", None), P("segment", "dp", None))
    return jax.shard_map(body, mesh=mesh, in_specs=in_specs, out_specs=out_specs, check_vma=False)
```

```python
import jax
import jax.numpy as jnp
from jax import lax
from jax.sharding import PartitionSpec as P

EPSILON = 1e-06
BF16 = jnp.bfloat16
F32 = jnp.float32
LANES = 128

GATE_SHARE = 1.0
UP_SHARE = 0.0
EARLY_HIDDEN_SHARE = 1.0
LATE_HIDDEN_SHARE = 1.0
EARLY_BACK_SHARE = 0.0
LATE_BACK_SHARE = 0.0
HOP_PIECES = 2


def cut(width, share):
    if share <= 0.0:
        return 0
    if share >= 1.0:
        return width
    whole = width // LANES
    return min(max(int(whole * share + 0.5), 1), whole - 1) * LANES


def pieces_of(low, high, count):
    units = (high - low) // LANES
    count = max(1, min(count, units))
    edges = [low + LANES * (units * i // count) for i in range(count)] + [high]
    return list(zip(edges[:-1], edges[1:]))


def contract_last(left, right):
    return lax.dot_general(left, right, (((1,), (1,)), ((), ())), preferred_element_type=F32)


def product(left, right):
    return jnp.dot(left, right, preferred_element_type=F32).astype(BF16)


def swap(value, axis, step=1):
    count = lax.axis_size(axis)
    return lax.ppermute(value, axis, [(i, i ^ step) for i in range(count)])


def line_exchange(value):
    count = lax.axis_size("dp")
    groups = [list(range(start, count, 2)) for start in range(2)]
    return lax.all_to_all(
        value, "dp", split_axis=0, concat_axis=0, tiled=True, axis_index_groups=groups
    )


def is_first_of_pair():
    return lax.axis_index("dp") % 2 == 0


def to_relative(value):
    count = lax.axis_size("dp")
    split = value.reshape((count // 2, 2, value.shape[0] // count) + value.shape[1:])
    flat = (value.shape[0] // 2,) + value.shape[1:]
    first, second = split[:, 0].reshape(flat), split[:, 1].reshape(flat)
    here = is_first_of_pair()
    return jnp.where(here, first, second), jnp.where(here, second, first)


def from_relative(own, other):
    count = lax.axis_size("dp")
    here = is_first_of_pair()
    shape = (count // 2, own.shape[0] // (count // 2)) + own.shape[1:]
    first = jnp.where(here, own, other).reshape(shape)
    second = jnp.where(here, other, own).reshape(shape)
    return jnp.stack([first, second], axis=1).reshape((2 * own.shape[0],) + own.shape[1:])


def scatter_product(multiply, values, width, share, marks=None, before=None):
    half_count = lax.axis_size("dp") // 2
    edge = cut(width, share)
    outs = []
    if edge > 0:
        part = multiply(values, 0, edge)
        if marks is not None:
            marks.append(part)
        if before is not None:
            part, before = lax.optimization_barrier((part, before))
        outs.append(lax.psum_scatter(part, "dp", scatter_dimension=0, tiled=True).astype(F32))
    if edge < width:
        own, other = to_relative(values)
        for low, high in pieces_of(edge, width, HOP_PIECES):
            given = multiply(other, low, high)
            own, given = lax.optimization_barrier((own, given))
            kept = lax.optimization_barrier(multiply(own, low, high))
            if marks is not None:
                marks.append(kept)
            paired = (kept.astype(F32) + swap(given, "dp").astype(F32)).astype(BF16)
            lined = line_exchange(paired.reshape(half_count, -1, high - low))
            outs.append(jnp.sum(lined.astype(F32), axis=0))
    return jnp.concatenate(outs, axis=1) if len(outs) > 1 else outs[0]


def gather_contract(multiply, value, share, extra=None, first=None, marks=None):
    half_count = lax.axis_size("dp") // 2
    width = value.shape[1]
    edge = cut(width, share)
    total = None
    everyone = None
    if edge < width:
        own_total, other_total = None, None
        for low, high in pieces_of(edge, width, HOP_PIECES):
            part = value[:, low:high]
            if extra is not None and low == edge:
                part = jnp.concatenate([part, extra], axis=1)
            lined = line_exchange(jnp.broadcast_to(part[None], (half_count,) + part.shape))
            lined = lined.reshape(-1, part.shape[1])
            arrived = swap(lined, "dp")
            if own_total is not None:
                lined, own_total = lax.optimization_barrier((lined, own_total))
            if extra is not None and low == edge:
                everyone = from_relative(lined[:, high - low :], arrived[:, high - low :])
                lined, arrived = lined[:, : high - low], arrived[:, : high - low]
            own_part = multiply(lined, low, high)
            if first is not None and high == width:
                arrived, first = lax.optimization_barrier((arrived, first))
            other_part = multiply(arrived, low, high)
            own_total = own_part if own_total is None else own_total + own_part
            other_total = other_part if other_total is None else other_total + other_part
        total = from_relative(own_total, other_total)
    if edge > 0:
        part = value[:, :edge]
        if extra is not None and edge == width:
            part = jnp.concatenate([part, extra], axis=1)
        called = lax.all_gather(part, "dp", axis=0, tiled=True)
        if marks is not None:
            marks.append(called)
        if extra is not None and edge == width:
            everyone = called[:, edge:]
        called = multiply(called[:, :edge], 0, edge)
        total = called if total is None else total + called
    if first is not None:
        total = total + first
    return total, everyone


def halving_sum(value, axis):
    step = 1
    while step < lax.axis_size(axis):
        value = value + swap(value, axis, step)
        step *= 2
    return value


def sum_shares(partial_value):
    total = partial_value.astype(BF16)
    total = (total.astype(F32) + swap(total, "segment").astype(F32)).astype(BF16)
    step = 1
    while step < lax.axis_size("tensor"):
        total = (total.astype(F32) + swap(total, "tensor", step).astype(F32)).astype(BF16)
        step *= 2
    return total.astype(F32)


def input_grads(d_hidden, stash_gate, stash_up):
    gate_pre = stash_gate.astype(F32)
    up_pre = stash_up.astype(F32)
    sigmoid_gate = jax.nn.sigmoid(gate_pre)
    d_gate = (d_hidden * up_pre * sigmoid_gate * (1.0 + gate_pre * (1.0 - sigmoid_gate))).astype(BF16)
    d_up = (d_hidden * gate_pre * sigmoid_gate).astype(BF16)
    return (d_gate, d_up)


def body(tokens, cotangent, gains, w_gate, w_up, w_down):
    gate_weight, up_weight, down_weight = w_gate[0], w_up[0], w_down[0]
    column_block, held = gate_weight.shape
    half = held // 2
    rows, features = tokens.shape
    segment = lax.axis_index("segment")
    block = lax.axis_index("dp")
    leading = segment == 0

    def other_half(weight, position):
        given = lax.dynamic_slice_in_dim(weight, (1 - position) * half, half, 1)
        return swap(given, "segment")

    def half_pick(own, other, early, function):
        def apply(value, low, high):
            first = lambda v, mine, theirs: function(v, mine, low, high)
            if early:
                return lax.cond(
                    leading, first, lambda v, m, t: function(v, t, low, high), value, own, other
                )
            return lax.cond(
                leading,
                lambda v, m, t: function(v, t, low, high),
                lambda v, m, t: function(v, m, half + low, half + high),
                value,
                own,
                other,
            )

        return apply

    def columns_product(value, weight, low, high):
        return product(value, weight[:, low:high])

    def columns_contract(value, weight, low, high):
        return contract_last(value, weight[:, low:high])

    def own_rows(value):
        return lax.dynamic_slice_in_dim(value, block * rows, rows, 0)

    def to_rows(value):
        return lax.all_to_all(value, "dp", split_axis=0, concat_axis=1, tiled=True)

    def row_inverse(cols):
        wide = cols.astype(F32)
        total = halving_sum(jnp.sum(wide * wide, axis=1), "dp")
        return lax.rsqrt(total[:, None] / features + EPSILON)

    gate_other = other_half(gate_weight, segment)
    up_other = other_half(up_weight, segment)
    mixed = lax.all_to_all(
        jnp.where(leading, tokens, cotangent), "dp", split_axis=1, concat_axis=0, tiled=True
    )
    mixed_other = swap(mixed, "segment")
    token_cols = jnp.where(leading, mixed, mixed_other)
    cotangent_cols = jnp.where(leading, mixed_other, mixed)
    gain_own = lax.dynamic_slice_in_dim(gains, block * column_block, column_block, 1)
    gain_other = swap(gain_own, "segment")
    early_gain = jnp.where(leading, gain_own, gain_other)
    late_gain = jnp.where(leading, gain_other, gain_own)

    def gate_and_up(early, cols, gain_row, marks=None):
        scaled = (cols.astype(F32) * gain_row).astype(BF16)
        gate = scatter_product(
            half_pick(gate_weight, gate_other, early, columns_product), scaled, half, GATE_SHARE, marks
        )
        up = scatter_product(
            half_pick(up_weight, up_other, early, columns_product), scaled, half, UP_SHARE, marks
        )
        return gate, up

    def hidden_of(gate, up):
        return (jax.nn.silu(gate) * up).astype(BF16)

    def back(early, d_hidden, gate, up):
        d_gate, d_up = input_grads(d_hidden, gate.astype(BF16), up.astype(BF16))
        share = jnp.sum(d_gate.astype(F32) * gate + d_up.astype(F32) * up, axis=1, keepdims=True)
        high = share.astype(BF16)
        low = (share - high.astype(F32)).astype(BF16)
        extra = jnp.pad(jnp.concatenate([high, low], axis=1), ((0, 0), (0, LANES - 2)))
        by_gate, _ = gather_contract(
            half_pick(gate_weight, gate_other, early, columns_contract), d_gate, GATE_SHARE
        )
        d_normed, everyone = gather_contract(
            half_pick(up_weight, up_other, early, columns_contract), d_up, UP_SHARE, extra, by_gate
        )
        shares = jnp.sum(everyone[:, :2].astype(F32), axis=1)
        mean_value = halving_sum(halving_sum(shares, "segment"), "tensor")[:, None] / features
        return d_normed, mean_value

    def norm_back(cols, inverse, gain_row, d_normed, mean_value, incoming):
        unit = cols.astype(F32) * inverse
        weighted = d_normed * gain_row
        return (incoming.astype(F32) + inverse * (weighted - unit * mean_value)).astype(BF16)

    inverse_in = row_inverse(token_cols)
    marks = []
    early_gate, early_up = gate_and_up(True, token_cols, early_gain, marks)
    after, _ = lax.optimization_barrier((segment, tuple(marks)))
    down_other = other_half(down_weight, after)
    late_d_hidden = scatter_product(
        half_pick(down_weight, down_other, False, columns_product),
        cotangent_cols,
        half,
        LATE_BACK_SHARE,
    )
    early_gate, early_up = early_gate * own_rows(inverse_in), early_up * own_rows(inverse_in)
    down_out, _ = gather_contract(
        half_pick(down_weight, down_other, True, columns_contract),
        hidden_of(early_gate, early_up),
        EARLY_HIDDEN_SHARE,
    )
    early_out = (token_cols.astype(F32) + sum_shares(down_out)).astype(BF16)
    early_out, late_d_hidden = lax.optimization_barrier((early_out, late_d_hidden))

    inverse_mid = row_inverse(early_out)
    late_gate, late_up = gate_and_up(False, early_out, late_gain)
    late_gate, late_up = late_gate * own_rows(inverse_mid), late_up * own_rows(inverse_mid)
    d_normed, mean_value = back(False, late_d_hidden, late_gate, late_up)
    down_out, _ = gather_contract(
        half_pick(down_weight, down_other, False, columns_contract),
        hidden_of(late_gate, late_up),
        LATE_HIDDEN_SHARE,
        marks=marks,
    )
    d_early = norm_back(
        early_out, inverse_mid, late_gain, sum_shares(d_normed), mean_value, cotangent_cols
    )
    late_out = (early_out.astype(F32) + sum_shares(down_out)).astype(BF16)
    acts = to_rows(jnp.where(leading, early_out, late_out))[None]

    d_hidden = scatter_product(
        half_pick(down_weight, down_other, True, columns_product),
        d_early,
        half,
        EARLY_BACK_SHARE,
        before=marks[-1],
    )
    d_normed, mean_value = back(True, d_hidden, early_gate, early_up)
    d_tokens = norm_back(
        token_cols, inverse_in, early_gain, sum_shares(d_normed), mean_value, d_early
    )
    grads = to_rows(jnp.where(leading, d_tokens, d_early))[None]
    return (acts, grads)


def solution(mesh):
    in_specs = (
        P("dp", None),
        P("dp", None),
        P("segment", None),
        P("segment", "dp", "tensor"),
        P("segment", "dp", "tensor"),
        P("segment", "dp", "tensor"),
    )
    out_specs = (P("segment", "dp", None), P("segment", "dp", None))
    return jax.shard_map(body, mesh=mesh, in_specs=in_specs, out_specs=out_specs, check_vma=False)
```
